512 devices in a mesh: tm: 32 (over y, z_hi, core), space: 16 (over x, z_lo).
Axes of the slice: x: 4, y: 8, z: 8 (z_hi: 2, z_lo: 4; z = z_hi * 4 + z_lo), core: 2. Of those that a mesh axis runs over, the one named last changes fastest.
Arguments:
- queries: bfloat16 [64, 1024, 2048], P('tm', 'space'), may hold values from -6 to 6
- keys: bfloat16 [64, 1024, 2048], P('tm', 'space'), may hold values from -6 to 6
- values: bfloat16 [64, 1024, 2048], P('tm', 'space'), may hold values from -6 to 6
- d_queries: bfloat16 [64, 1024, 2048], P('tm', 'space'), may hold values from -6 to 6
- d_keys: bfloat16 [64, 1024, 2048], P('tm', 'space'), may hold values from -6 to 6
- d_values: bfloat16 [64, 1024, 2048], P('tm', 'space'), may hold values from -6 to 6
Outputs:
- combined: bfloat16 [64, 1024, 2048], P('tm', 'space')
- d_combined: bfloat16 [64, 1024, 2048], P('tm', 'space')
The draws below stay inside these ranges and needn't reach their ends.
All inputs are finite; a program needn't handle non-finite values.
Results may differ from the reference program's by a relative error of at most 0.0058.
Values may be sent and summed in bfloat16 or wider, within the bound.
No kernel may reach another device: no remote copies, remote signals or barrier semaphores. Data moves between devices by JAX's collectives and lax.ppermute only.
A program may use at most 64 MiB of HBM per device.

```python
import jax
import jax.numpy as jnp
from jax import lax

HEADS = 32
HEAD_DIM = 64
TOK_FRAME = 1024
WIDTH = 2048
FRAMES = 64


def draw_queries(key, part):
    key = jax.random.fold_in(key, 1)
    drawn = jnp.clip(jax.random.normal(key, (FRAMES, TOK_FRAME, HEADS, HEAD_DIM), jnp.float32), -6.0, 6.0)
    return drawn.reshape(FRAMES, TOK_FRAME, WIDTH).astype(jnp.bfloat16)


def draw_keys(key, part):
    key = jax.random.fold_in(key, 2)
    drawn = jnp.clip(jax.random.normal(key, (FRAMES, TOK_FRAME, HEADS, HEAD_DIM), jnp.float32), -6.0, 6.0)
    return drawn.reshape(FRAMES, TOK_FRAME, WIDTH).astype(jnp.bfloat16)


def shard_levels(key, extent, pieces, smallest, high):
    def one(position, shards_of):
        heights = jax.random.uniform(jax.random.fold_in(jax.random.fold_in(key, 6), position), (shards_of,), jnp.float32, smallest / len(pieces), high / len(pieces))
        return jnp.repeat(jnp.exp(heights), extent[position] // shards_of).reshape((-1,) + (1,) * (len(extent) - position - 1))

    gain = one(*pieces[0])
    for cut in pieces[1:]:
        gain = gain * one(*cut)
    return gain


def gaussian(key, extent, scale, reach, shards=(), dtype=jnp.bfloat16):
    array = scale * jax.random.normal(key, extent, jnp.float32)
    if shards:
        array = array * shard_levels(key, extent, shards, -0.22, 0.18)
    return jnp.clip(array, -reach, reach).astype(dtype)


def setup_inputs(seed: int = 0) -> dict:
    key_of = jax.random.split(jax.random.key(seed), 7)
    return {
        "queries": draw_queries(jax.random.fold_in(key_of[6], 71), 0),
        "keys": draw_keys(jax.random.fold_in(key_of[6], 71), 0),
        "values": gaussian(key_of[2], (FRAMES, TOK_FRAME, WIDTH), 1.0, 6.0, ((0, 32), (1, 16))),
        "d_queries": gaussian(key_of[3], (FRAMES, TOK_FRAME, WIDTH), 1.0, 6.0, ((0, 32), (1, 16))),
        "d_keys": gaussian(key_of[4], (FRAMES, TOK_FRAME, WIDTH), 1.0, 6.0, ((0, 32), (1, 16))),
        "d_values": gaussian(key_of[5], (FRAMES, TOK_FRAME, WIDTH), 1.0, 6.0, ((0, 32), (1, 16))),
    }


def attend(query_rows, key_rows, value_rows, d_query, d_key, d_value):
    score_scale = HEAD_DIM ** -0.5
    scores = jnp.dot(query_rows, key_rows.T, preferred_element_type=jnp.float32) * score_scale
    tangent = (jnp.dot(d_query, key_rows.T, preferred_element_type=jnp.float32)
               + jnp.dot(query_rows, d_key.T, preferred_element_type=jnp.float32)) * score_scale
    highest = jnp.max(scores, axis=-1, keepdims=True)
    weights = jnp.exp(scores - highest)
    probabilities = weights / jnp.sum(weights, axis=-1, keepdims=True)
    d_probabilities = probabilities * (tangent - jnp.sum(probabilities * tangent, axis=-1, keepdims=True))
    probs_low = probabilities.astype(jnp.bfloat16)
    d_low = d_probabilities.astype(jnp.bfloat16)
    output = jnp.dot(probs_low, value_rows, preferred_element_type=jnp.float32)
    d_output = (jnp.dot(d_low, value_rows, preferred_element_type=jnp.float32)
                + jnp.dot(probs_low, d_value, preferred_element_type=jnp.float32))
    return output.astype(jnp.bfloat16), d_output.astype(jnp.bfloat16)


def by_frame(member):
    shaped = member.reshape(FRAMES, TOK_FRAME, HEADS, HEAD_DIM).transpose(0, 2, 1, 3)
    return shaped.reshape(FRAMES * HEADS, TOK_FRAME, HEAD_DIM)


def from_frame(member):
    shaped = member.reshape(FRAMES, HEADS, TOK_FRAME, HEAD_DIM).transpose(0, 2, 1, 3)
    return shaped.reshape(FRAMES, TOK_FRAME, WIDTH)


def by_token(member):
    return member.reshape(FRAMES, TOK_FRAME, HEADS, HEAD_DIM).transpose(1, 2, 0, 3)


def from_token(member):
    return member.transpose(2, 0, 1, 3).reshape(FRAMES, TOK_FRAME, WIDTH)


def reference(queries, keys, values, d_queries, d_keys, d_values):
    arrays = (queries, keys, values, d_queries, d_keys, d_values)
    spatial, d_spatial = lax.map(lambda members: attend(*members), tuple(by_frame(member) for member in arrays))
    temporal, d_temporal = lax.map(lambda members: jax.vmap(attend)(*members), tuple(by_token(member) for member in arrays))
    combined = (from_frame(spatial).astype(jnp.float32) + from_token(temporal).astype(jnp.float32)).astype(jnp.bfloat16)
    d_combined = (from_frame(d_spatial).astype(jnp.float32) + from_token(d_temporal).astype(jnp.float32)).astype(jnp.bfloat16)
    return combined, d_combined
```

```python
import functools
import jax
import jax.numpy as jnp
from jax import lax
from jax.experimental import pallas as pl
from jax.experimental.pallas import tpu as pltpu
from jax.sharding import PartitionSpec as P

HEAD_DIM = 64
LANES = 128
F32 = jnp.float32
BF16 = jnp.bfloat16
VMEM_LIMIT = 50 * 1024 * 1024


def params():
    return pltpu.CompilerParams(vmem_limit_bytes=VMEM_LIMIT)


def dot_t(a, b):
    return lax.dot_general(a, b, (((1,), (1,)), ((), ())), preferred_element_type=F32)


def dot(a, b):
    return jnp.dot(a, b, preferred_element_type=F32)


def pack_space_kernel(*refs):
    out = refs[6]
    for a in range(6):
        out[0, a] = refs[a][...]


def pack_space(arrays):
    frames, tokens, width = arrays[0].shape
    pairs = width // LANES
    return pl.pallas_call(
        pack_space_kernel,
        grid=(pairs,),
        in_specs=[pl.BlockSpec((frames, tokens, LANES), lambda d: (0, 0, d))] * 6,
        out_specs=pl.BlockSpec((1, 6, frames, tokens, LANES), lambda d: (d, 0, 0, 0, 0)),
        out_shape=jax.ShapeDtypeStruct((pairs, 6, frames, tokens, LANES), BF16),
        compiler_params=params(),
        cost_estimate=pl.CostEstimate(flops=0, bytes_accessed=6 << 20, transcendentals=0),
        name="pack_space",
    )(*arrays)


def pack_time_kernel(*refs):
    out = refs[6]
    groups = out.shape[0]
    for a in range(6):
        for pair in range(2):
            for f in range(2):
                for g in range(groups):
                    out[g, 0, a, pair, f] = refs[a][f, g * 16:(g + 1) * 16, pair * LANES:(pair + 1) * LANES]


def pack_time(arrays):
    frames, tokens, width = arrays[0].shape
    groups, lane_groups = tokens // 16, width // 256
    return pl.pallas_call(
        pack_time_kernel,
        grid=(lane_groups,),
        in_specs=[pl.BlockSpec((frames, tokens, 256), lambda d: (0, 0, d))] * 6,
        out_specs=pl.BlockSpec((groups, 1, 6, 2, frames, 16, LANES), lambda d: (0, d, 0, 0, 0, 0, 0)),
        out_shape=jax.ShapeDtypeStruct((groups, lane_groups, 6, 2, frames, 16, LANES), BF16),
        compiler_params=params(),
        cost_estimate=pl.CostEstimate(flops=0, bytes_accessed=6 << 20, transcendentals=0),
        name="pack_time",
    )(*arrays)


def soft_parts(s, ds):
    e = jnp.exp(s - jnp.max(s, axis=-1, keepdims=True))
    p = e * (1.0 / jnp.sum(e, axis=-1, keepdims=True))
    dp = p * (ds - jnp.sum(p * ds, axis=-1, keepdims=True))
    return p.astype(BF16), dp.astype(BF16)


def spatial_kernel(q_ref, dq_ref, k_ref, v_ref, dk_ref, dv_ref, out_ref):
    rows = q_ref.shape[0] * q_ref.shape[3]
    keys = k_ref.shape[0] * k_ref.shape[3]
    q = q_ref[...].reshape(rows, LANES)
    dq = dq_ref[...].reshape(rows, LANES)
    k = k_ref[...].reshape(keys, LANES)
    v = v_ref[...].reshape(keys, LANES)
    dk = dk_ref[...].reshape(keys, LANES)
    dv = dv_ref[...].reshape(keys, LANES)
    kk = jnp.concatenate([k, dk], axis=-1)
    vv = jnp.concatenate([v, dv], axis=-1)
    lane = lax.broadcasted_iota(jnp.int32, (1, LANES), 1)
    low = lane < HEAD_DIM
    results = []
    for head in range(2):
        scale = jnp.where(low == (head == 0), HEAD_DIM ** -0.5, 0.0).astype(BF16)
        qh = q * scale
        dqh = dq * scale
        s = dot_t(qh, k)
        ds = dot_t(jnp.concatenate([dqh, qh], axis=-1), kk)
        p, dp = soft_parts(s, ds)
        both = dot(p, vv)
        results.append((both[:, :LANES], both[:, LANES:] + dot(dp, v)))
    shape = out_ref.shape[:1] + out_ref.shape[3:]
    for i in range(2):
        value = jnp.where(low, results[0][i], results[1][i]).astype(BF16)
        out_ref[:, i, 0] = value.reshape(shape)


def spatial(x, blocks=2):
    sources, _, frames, tokens, _ = x.shape
    per = sources // blocks

    def q_spec(a):
        return pl.BlockSpec((per, 1, 1, tokens, LANES), lambda f, b: (b, a, f, 0, 0))

    def k_spec(a):
        return pl.BlockSpec((sources, 1, 1, tokens, LANES), lambda f, b: (0, a, f, 0, 0))

    return pl.pallas_call(
        spatial_kernel,
        grid=(frames, blocks),
        in_specs=[q_spec(0), q_spec(3), k_spec(1), k_spec(2), k_spec(4), k_spec(5)],
        out_specs=pl.BlockSpec((per, 2, 1, tokens, LANES), lambda f, b: (b, 0, f, 0, 0)),
        out_shape=jax.ShapeDtypeStruct((sources, 2, frames, tokens, LANES), BF16),
        compiler_params=params(),
        cost_estimate=pl.CostEstimate(flops=9 << 30, bytes_accessed=4 << 20, transcendentals=4 << 20),
        name="spatial",
    )(*([x] * 6))


def temporal_kernel(x_ref, out_ref):
    sources = x_ref.shape[0]
    parts = sources // 8
    r_out = lax.broadcasted_iota(jnp.int32, (256, 256), 0)
    r_in = lax.broadcasted_iota(jnp.int32, (256, 256), 1)
    t_of, s_of, f_of = r_out // 16, (r_out % 16) // 2, r_out % 2
    gather = jnp.where(r_in == s_of * 32 + f_of * 16 + t_of, 1.0, 0.0).astype(BF16)
    t_at, s_at, f_at = r_in // 16, (r_in % 16) // 2, r_in % 2
    scatter = jnp.where(r_out == s_at * 32 + f_at * 16 + t_at, 1.0, 0.0).astype(BF16)
    members = []
    for a in range(6):
        members.append([x_ref[8 * i:8 * i + 8, a, 0].reshape(256, LANES) for i in range(parts)])
    moved = []
    for i in range(parts):
        rows = jnp.concatenate([members[a][i] for a in range(6)], axis=-1)
        moved.append(dot(gather, rows).astype(BF16))
    lane = lax.broadcasted_iota(jnp.int32, (1, LANES), 1)
    low = lane < HEAD_DIM
    scale0 = jnp.where(low, HEAD_DIM ** -0.5, 0.0).astype(BF16)
    scale1 = jnp.where(low, 0.0, HEAD_DIM ** -0.5).astype(BF16)
    row = lax.broadcasted_iota(jnp.int32, (256, LANES), 0)
    col = lax.broadcasted_iota(jnp.int32, (256, LANES), 1)
    same = ((row // 64) % 2) == (col // 64)
    pieces = [[], []]
    for g in range(8):
        tokens = (2 * g, 2 * g + 1)
        block = jnp.concatenate(
            [moved[i][t * 16:(t + 1) * 16] for t in tokens for i in range(parts)], axis=0)
        q, k, v, dq, dk, dv = [block[:, a * LANES:(a + 1) * LANES] for a in range(6)]
        qh = jnp.concatenate([q * scale0, q * scale1], axis=0)
        dqh = jnp.concatenate([dq * scale0, dq * scale1], axis=0)
        s = jnp.where(same, dot_t(qh, k), -jnp.inf)
        ds = dot_t(jnp.concatenate([dqh, qh], axis=-1), jnp.concatenate([k, dk], axis=-1))
        p, dp = soft_parts(s, ds)
        both = dot(p, jnp.concatenate([v, dv], axis=-1))
        o, do = both[:, :LANES], both[:, LANES:] + dot(dp, v)
        pieces[0].append(jnp.where(low, o[:LANES], o[LANES:]).astype(BF16))
        pieces[1].append(jnp.where(low, do[:LANES], do[LANES:]).astype(BF16))
    for i in range(parts):
        sides = []
        for side in range(2):
            sides.append(jnp.concatenate(
                [pieces[side][t // 2][(t % 2) * 64 + i * 16:(t % 2) * 64 + i * 16 + 16] for t in range(16)], axis=0))
        back = dot(scatter, jnp.concatenate(sides, axis=-1)).astype(BF16)
        for side in range(2):
            out_ref[8 * i:8 * i + 8, side, 0] = back[:, side * LANES:(side + 1) * LANES].reshape(8, 2, 16, LANES)


def temporal(x):
    sources, _, pairs, frames, tokens, _ = x.shape
    return pl.pallas_call(
        temporal_kernel,
        grid=(pairs,),
        in_specs=[pl.BlockSpec((sources, 6, 1, frames, tokens, LANES), lambda h: (0, 0, h, 0, 0, 0))],
        out_specs=pl.BlockSpec((sources, 2, 1, frames, tokens, LANES), lambda h: (0, 0, h, 0, 0, 0)),
        out_shape=jax.ShapeDtypeStruct((sources, 2, pairs, frames, tokens, LANES), BF16),
        compiler_params=params(),
        cost_estimate=pl.CostEstimate(flops=4 << 30, bytes_accessed=4 << 20, transcendentals=1 << 20),
        name="temporal",
    )(x)


def combine_kernel(s_ref, t_ref, out_ref, d_out_ref):
    groups = t_ref.shape[0]
    for i, ref in ((0, out_ref), (1, d_out_ref)):
        for pair in range(2):
            for f in range(2):
                for g in range(groups):
                    a = s_ref[pair, i, f, g * 16:(g + 1) * 16].astype(F32)
                    b = t_ref[g, 0, i, pair, f].astype(F32)
                    ref[f, g * 16:(g + 1) * 16, pair * LANES:(pair + 1) * LANES] = (a + b).astype(BF16)


def combine(s, t):
    pairs, _, frames, tokens, _ = s.shape
    groups, lane_groups = t.shape[:2]
    shape = jax.ShapeDtypeStruct((frames, tokens, pairs * LANES), BF16)
    spec = pl.BlockSpec((frames, tokens, 256), lambda d: (0, 0, d))
    return pl.pallas_call(
        combine_kernel,
        grid=(lane_groups,),
        in_specs=[
            pl.BlockSpec((2, 2, frames, tokens, LANES), lambda d: (d, 0, 0, 0, 0)),
            pl.BlockSpec((groups, 1, 2, 2, frames, 16, LANES), lambda d: (0, d, 0, 0, 0, 0, 0)),
        ],
        out_specs=[spec, spec],
        out_shape=[shape, shape],
        compiler_params=params(),
        cost_estimate=pl.CostEstimate(flops=0, bytes_accessed=3 << 20, transcendentals=0),
        name="combine",
    )(s, t)


def swap(x, axis):
    return lax.all_to_all(x, axis, split_axis=0, concat_axis=0, tiled=True)


def body(*arrays):
    space_in = swap(pack_space(arrays), "space")
    packed = pack_time(arrays)
    shape = packed.shape
    time_in = swap(packed.reshape((shape[0] * shape[1],) + shape[2:]), "tm")
    space_out = swap(spatial(space_in), "space")
    time_out = swap(temporal(time_in), "tm")
    return tuple(combine(space_out, time_out.reshape(shape[:2] + (2,) + shape[3:])))


def solution(mesh):
    spec = P("tm", "space", None)
    return jax.shard_map(
        body, mesh=mesh, in_specs=(spec,) * 6, out_specs=(spec,) * 2, check_vma=False)
```

```python
import jax
import jax.numpy as jnp
import numpy as np
from jax import lax
from jax.experimental import pallas as pl
from jax.experimental.pallas import tpu as pltpu
from jax.sharding import PartitionSpec as P

HEAD_DIM = 64
LANES = 128
F32 = jnp.float32
BF16 = jnp.bfloat16
VMEM_LIMIT = 50 * 1024 * 1024
COST = pl.CostEstimate(flops=0, bytes_accessed=1024, transcendentals=0)


def dot_t(a, b):
    return lax.dot_general(a, b, (((1,), (1,)), ((), ())), preferred_element_type=F32)


def dot(a, b):
    return jnp.dot(a, b, preferred_element_type=F32)


MESH = (8, 2, 2, 4, 4)
AXES = ("tm", "space")
ROW = (64, LANES)


def groups_of(kind, core):
    ids = np.arange(512).reshape(MESH)[:, :, core]
    if kind == "space":
        found = [ids[y, zh].reshape(-1) for y in range(8) for zh in range(2)]
    elif kind == "time":
        found = [ids[:, :, x, z].reshape(-1) for x in range(4) for z in range(4)]
    else:
        found = [np.stack([ids[:, 0, x, z], ids[:, 1, x, z ^ 3]], axis=1).reshape(-1)
                 for x in range(4) for z in range(4)]
    return [[int(i) for i in group] for group in found]


def exchange(value, first, second):
    return lax.all_to_all(
        value, AXES, split_axis=0, concat_axis=0, tiled=True,
        axis_index_groups=groups_of(first, 0) + groups_of(second, 1))


def swap_cores(value):
    ids = np.arange(512).reshape(MESH)
    pairs = zip(ids.reshape(-1), ids[:, :, ::-1].reshape(-1))
    return lax.ppermute(value, AXES, [(int(a), int(b)) for a, b in pairs])


def call(kernel, scalars, operands, grid, in_specs, out_specs, out_shape, name, **kwargs):
    return pl.pallas_call(
        kernel,
        grid_spec=pltpu.PrefetchScalarGridSpec(
            num_scalar_prefetch=1, grid=grid, in_specs=in_specs, out_specs=out_specs),
        out_shape=out_shape,
        cost_estimate=COST,
        name=name,
        **kwargs,
    )(scalars, *operands)


def out_like(*shape):
    return jax.ShapeDtypeStruct(shape, BF16)


def swap_lanes():
    row = lax.broadcasted_iota(jnp.int32, (256, 256), 0)
    col = lax.broadcasted_iota(jnp.int32, (256, 256), 1)
    block = col // 64
    source = jnp.where(block == 1, col + 64, jnp.where(block == 2, col - 64, col))
    return jnp.where(row == source, 1.0, 0.0).astype(BF16)


def shift_lanes(down):
    row = lax.broadcasted_iota(jnp.int32, (LANES, LANES), 0)
    col = lax.broadcasted_iota(jnp.int32, (LANES, LANES), 1)
    return jnp.where(row == col + (64 if down else -64), 1.0, 0.0).astype(BF16)


def pack_rows(s, refs, out):
    swap = swap_lanes()
    rows = [
        jnp.concatenate(
            [refs[m][:, :, pair * LANES:(pair + 1) * LANES].reshape(128, LANES) for m in members], axis=-1)
        for pair in range(2) for members in ((3, 0), (1, 4), (2, 5))]
    rows = dot(jnp.concatenate(rows, axis=0), swap).astype(BF16)
    for pair in range(2):
        for a in range(3):
            for half in range(2):
                out[(2 * pair + half) ^ s[1], a] = (
                    rows[(3 * pair + a) * 128:(3 * pair + a + 1) * 128, half * LANES:(half + 1) * LANES]
                    .reshape(2, 64, LANES))


def pack_own(scalars, arrays):
    def kernel(s, *refs):
        pack_rows(s, refs[:6], refs[6])

    return call(
        kernel, scalars, arrays, (4,),
        [pl.BlockSpec((2, 64, 256), lambda n, s: (0, 0, 4 * s[0] + n))] * 6,
        pl.BlockSpec((4, 3, 2) + ROW, lambda n, s: (n, 0, 0, 0, 0)),
        out_like(16, 3, 4, *ROW), "pack_own")


def pack_other(scalars, own, other):
    def kernel(s, *refs):
        pack_rows(s, refs[:6], refs[7])

    def spec(a):
        return pl.BlockSpec((None, 2, 64, 256), lambda n, s: (a, 0, 0, n))

    return call(
        kernel, scalars, [other] * 6 + [own], (4,),
        [spec(a) for a in range(6)] + [pl.BlockSpec(memory_space=pl.ANY)],
        pl.BlockSpec((4, 3, 2) + ROW, lambda n, s: (n, 0, 1, 0, 0)),
        out_like(*own.shape), "pack_other", input_output_aliases={7: 0})


def other_heads(scalars, arrays):
    def kernel(s, *refs):
        for a in range(6):
            refs[6][a] = refs[a][...]

    return call(
        kernel, scalars, arrays, (2,),
        [pl.BlockSpec((2, 64, 512), lambda n, s: (0, 0, 2 * (1 - s[0]) + n))] * 6,
        pl.BlockSpec((6, 2, 64, 512), lambda n, s: (0, 0, 0, n)),
        out_like(6, 2, 64, 1024), "other_heads")


def choose(scalars, first, second):
    def kernel(s, first_ref, second_ref, out_ref):
        @pl.when(s[0] == 0)
        def _():
            out_ref[...] = first_ref[...]

        @pl.when(s[0] == 1)
        def _():
            out_ref[...] = second_ref[...]

    block = (4, 3, 4) + ROW
    return call(
        kernel, scalars, [first, second], (4,),
        [pl.BlockSpec(block, lambda n, s: (n * (1 - s[0]), 0, 0, 0, 0)),
         pl.BlockSpec(block, lambda n, s: (n * s[0], 0, 0, 0, 0))],
        pl.BlockSpec(block, lambda n, s: (n, 0, 0, 0, 0)),
        out_like(*first.shape), "choose")


def soft_parts(s, ds):
    e = jnp.exp(s - jnp.max(s, axis=-1, keepdims=True))
    p = e * (1.0 / jnp.sum(e, axis=-1, keepdims=True))
    dp = p * (ds - jnp.sum(p * ds, axis=-1, keepdims=True))
    return p.astype(BF16), dp.astype(BF16)


def spatial_kernel(x_ref, out_ref, q_both, q_low, values):
    block = pl.program_id(1)
    count = q_both.shape[0]

    @pl.when(block == 0)
    def _():
        q = x_ref[:, 0, 0].reshape(count, LANES) * BF16(HEAD_DIM ** -0.5)
        v = x_ref[:, 2, 0].reshape(count, LANES)
        q_both[...] = q
        q_low[...] = dot(q, shift_lanes(True)).astype(BF16)
        values[:count] = v
        values[count:] = dot(v, shift_lanes(False)).astype(BF16)

    rows = count // 2
    here = pl.ds(pl.multiple_of(block * rows, rows), rows)
    keys = x_ref[:, 1, 0].reshape(count, LANES)
    s = dot_t(q_low[here, :], keys)
    ds = dot_t(q_both[here, :], keys)
    found = dot(jnp.concatenate(soft_parts(s, ds), axis=-1), values[...]).astype(BF16)
    out_ref[:, 0] = found.reshape(8, 64, LANES)


def spatial(x):
    rows = pltpu.VMEM((1024, LANES), BF16)
    return pl.pallas_call(
        spatial_kernel,
        grid=(4, 2),
        in_specs=[pl.BlockSpec((16, 3, 1) + ROW, lambda f, b: (0, 0, f, 0, 0))],
        out_specs=pl.BlockSpec((8, 1) + ROW, lambda f, b: (b, f, 0, 0)),
        out_shape=out_like(16, 4, *ROW),
        scratch_shapes=[rows, rows, pltpu.VMEM((2048, LANES), BF16)],
        compiler_params=pltpu.CompilerParams(vmem_limit_bytes=VMEM_LIMIT),
        cost_estimate=COST,
        name="spatial",
    )(x)


def temporal_kernel(x_ref, out_ref):
    row = lax.broadcasted_iota(jnp.int32, (256, 256), 0)
    col = lax.broadcasted_iota(jnp.int32, (256, 256), 1)
    turn = jnp.where(col == (row % 16) * 16 + row // 16, 1.0, 0.0).astype(BF16)
    down, up = shift_lanes(True), shift_lanes(False)
    moved = []
    for i in range(4):
        rows = jnp.concatenate([x_ref[4 * i:4 * i + 4, a].reshape(256, LANES) for a in range(3)], axis=-1)
        rows = dot(turn, rows).astype(BF16)
        q, k, v = [rows[:, a * LANES:(a + 1) * LANES] for a in range(3)]
        q = q * BF16(HEAD_DIM ** -0.5)
        moved.append((q, dot(q, down).astype(BF16), k, v, dot(v, up).astype(BF16)))
    row = lax.broadcasted_iota(jnp.int32, (LANES, LANES), 0)
    col = lax.broadcasted_iota(jnp.int32, (LANES, LANES), 1)
    same = (row // 64) == (col // 64)
    pieces = []
    for g in range(8):
        q, q_low, k, v, v_up = [
            jnp.concatenate(
                [moved[i][m][t * 16:(t + 1) * 16] for t in (2 * g, 2 * g + 1) for i in range(4)], axis=0)
            for m in range(5)]
        scores = dot_t(jnp.concatenate([q_low, q], axis=0), k)
        p, dp = soft_parts(jnp.where(same, scores[:LANES], -jnp.inf), scores[LANES:])
        found = dot(jnp.concatenate([p, dp], axis=-1), jnp.concatenate([v, v_up], axis=0))
        pieces.append(found.astype(BF16))
    back = []
    for i in range(4):
        back.append(jnp.concatenate(
            [pieces[t // 2][(t % 2) * 64 + i * 16:(t % 2) * 64 + i * 16 + 16] for t in range(16)], axis=0))
    back = dot(turn, jnp.concatenate(back, axis=-1)).astype(BF16)
    for i in range(4):
        out_ref[4 * i:4 * i + 4] = back[:, i * LANES:(i + 1) * LANES].reshape(4, 4, 16, LANES)


def temporal(x):
    return pl.pallas_call(
        temporal_kernel,
        grid=(4,),
        in_specs=[pl.BlockSpec((16, 3, 4, 16, LANES), lambda t: (0, 0, 0, t, 0))],
        out_specs=pl.BlockSpec((16, 4, 16, LANES), lambda t: (0, 0, t, 0)),
        out_shape=out_like(16, 4, *ROW),
        compiler_params=pltpu.CompilerParams(vmem_limit_bytes=VMEM_LIMIT),
        cost_estimate=COST,
        name="temporal",
    )(x)


def add_round(a, b):
    return (a.astype(F32) + b.astype(F32)).astype(BF16)


def add_in_plane(scalars, plane, value, extra, frames, *after):
    def kernel(s, value_ref, extra_ref, *refs):
        out_ref = refs[-1]
        both = add_round(value_ref[...], extra_ref[...])
        out_ref[...] = jnp.where(s[0] == plane, both, value_ref[...])

    block = (8, 4 if frames is None else 2) + ROW
    spec = pl.BlockSpec(block, lambda n, s: (n, frames or 0, 0, 0))
    return call(
        kernel, scalars, [value, extra, *after], (2,),
        [spec, spec] + [pl.BlockSpec(memory_space=pl.ANY)] * len(after),
        pl.BlockSpec(block, lambda n, s: (n, 0, 0, 0)), out_like(16, *block[1:]), "add_in_plane")


def finish(scalars, value, extra, other):
    def kernel(s, value_ref, extra_ref, other_ref, out_ref, d_out_ref):
        swap = swap_lanes()
        side = pl.program_id(0) // 2
        flip = jnp.where(side == 0, s[1], s[2])
        rows = []
        for pair in range(4):
            halves = []
            for half in range(2):
                d = (2 * pair + half) ^ flip
                own = value_ref[d].reshape(128, LANES)
                own = jnp.where(s[0] == 1, add_round(own, extra_ref[d].reshape(128, LANES)), own)
                halves.append(jnp.where(side == 0, own, other_ref[d].reshape(128, LANES)))
            rows.append(jnp.concatenate(halves, axis=-1))
        rows = dot(jnp.concatenate(rows, axis=0), swap).astype(BF16)
        for pair in range(4):
            for i, ref in ((0, out_ref), (1, d_out_ref)):
                ref[:, :, pair * LANES:(pair + 1) * LANES] = (
                    rows[128 * pair:128 * pair + 128, i * LANES:(i + 1) * LANES].reshape(2, 64, LANES))

    block = (8, 2) + ROW
    own = pl.BlockSpec(block, lambda n, s: (jnp.minimum(n, 1), 0, 0, 0))
    result = pl.BlockSpec((2, 64, 512), lambda n, s: (0, 0, 2 * ((n // 2) ^ s[0]) + n % 2))
    return call(
        kernel, scalars, [value, extra, other], (4,),
        [own, own, pl.BlockSpec(block, lambda n, s: (jnp.maximum(n - 2, 0), 0, 0, 0))],
        [result, result], [out_like(2, 64, 2048)] * 2, "finish")


def body(*arrays):
    arrays = list(arrays)
    time = lax.axis_index("tm")
    core, zh3 = time % 2, 3 * ((time // 2) % 2)
    scalars = jnp.stack([core, zh3 * (1 - core), zh3 * core]).astype(jnp.int32)
    other = swap_cores(other_heads(scalars, arrays))
    packed = pack_other(scalars, pack_own(scalars, arrays), other)
    first = exchange(packed, "space", "time")
    chosen, passed = lax.optimization_barrier((choose(scalars, first, packed), swap_cores(first[0, 0, 0, :16])))
    second = exchange(chosen, "mirrored", "space")
    early = lax.cond(core == 0, spatial, temporal, first)
    in_time = lax.cond(core == 0, lambda x, done: temporal(x), lambda x, done: done, second, early)
    in_space = lax.cond(core == 0, lambda x, done: done, lambda x, done: spatial(x), second, early)
    third = exchange(in_time, "mirrored", "time")
    fourth = exchange(add_in_plane(scalars, 0, in_space, third, None, passed), "space", "space")
    other = swap_cores(add_in_plane(scalars, 1, fourth, third, 1))
    return tuple(finish(scalars, fourth, third, other))


def solution(mesh):
    spec = P("tm", "space", None)
    return jax.shard_map(
        body, mesh=mesh, in_specs=(spec,) * 6, out_specs=(spec,) * 2, check_vma=False)
```

```python
import jax
import jax.numpy as jnp
import numpy as np
from jax import lax
from jax.experimental import pallas as pl
from jax.experimental.pallas import tpu as pltpu
from jax.sharding import PartitionSpec as P

HEAD_DIM = 64
LANES = 128
F32 = jnp.float32
BF16 = jnp.bfloat16
VMEM_LIMIT = 50 * 1024 * 1024
COST = pl.CostEstimate(flops=0, bytes_accessed=1024, transcendentals=0)


def dot_t(a, b):
    return lax.dot_general(a, b, (((1,), (1,)), ((), ())), preferred_element_type=F32)


def dot(a, b):
    return jnp.dot(a, b, preferred_element_type=F32)


MESH = (8, 2, 2, 4, 4)
AXES = ("tm", "space")
ROW = (64, LANES)


def groups_of(kind, core):
    ids = np.arange(512).reshape(MESH)[:, :, core]
    if kind == "space":
        found = [ids[y, zh].reshape(-1) for y in range(8) for zh in range(2)]
    else:
        found = [np.stack([ids[:, 0, x, z], ids[:, 1, x, z ^ 3]], axis=1).reshape(-1)
                 for x in range(4) for z in range(4)]
    return [[int(i) for i in group] for group in found]


def exchange(value, kind):
    return lax.all_to_all(
        value, AXES, split_axis=0, concat_axis=0, tiled=True,
        axis_index_groups=groups_of(kind, 0) + groups_of(kind, 1))


def swap_cores(value):
    ids = np.arange(512).reshape(MESH)
    pairs = zip(ids.reshape(-1), ids[:, :, ::-1].reshape(-1))
    return lax.ppermute(value, AXES, [(int(a), int(b)) for a, b in pairs])


def call(kernel, scalars, operands, grid, in_specs, out_specs, out_shape, name, **kwargs):
    return pl.pallas_call(
        kernel,
        grid_spec=pltpu.PrefetchScalarGridSpec(
            num_scalar_prefetch=1, grid=grid, in_specs=in_specs, out_specs=out_specs),
        out_shape=out_shape,
        cost_estimate=COST,
        name=name,
        **kwargs,
    )(scalars, *operands)


def out_like(*shape):
    return jax.ShapeDtypeStruct(shape, BF16)


def swap_lanes():
    row = lax.broadcasted_iota(jnp.int32, (256, 256), 0)
    col = lax.broadcasted_iota(jnp.int32, (256, 256), 1)
    block = col // 64
    source = jnp.where(block == 1, col + 64, jnp.where(block == 2, col - 64, col))
    return jnp.where(row == source, 1.0, 0.0).astype(BF16)


def shift_lanes(down):
    row = lax.broadcasted_iota(jnp.int32, (LANES, LANES), 0)
    col = lax.broadcasted_iota(jnp.int32, (LANES, LANES), 1)
    return jnp.where(row == col + (64 if down else -64), 1.0, 0.0).astype(BF16)


def pack_rows(s, refs, out):
    swap = swap_lanes()
    rows = [
        jnp.concatenate(
            [refs[m][:, :, pair * LANES:(pair + 1) * LANES].reshape(128, LANES) for m in members], axis=-1)
        for pair in range(2) for members in ((3, 0), (1, 4), (2, 5))]
    rows = dot(jnp.concatenate(rows, axis=0), swap).astype(BF16)
    for pair in range(2):
        for a in range(3):
            for half in range(2):
                out[(2 * pair + half) ^ s[1], a] = (
                    rows[(3 * pair + a) * 128:(3 * pair + a + 1) * 128, half * LANES:(half + 1) * LANES]
                    .reshape(2, 64, LANES))


def pack_own(scalars, arrays):
    def kernel(s, *refs):
        pack_rows(s, refs[:6], refs[6])

    return call(
        kernel, scalars, arrays, (4,),
        [pl.BlockSpec((2, 64, 256), lambda n, s: (0, 0, 4 * s[0] + n))] * 6,
        pl.BlockSpec((4, 3, 2) + ROW, lambda n, s: (n, 0, 0, 0, 0)),
        out_like(16, 3, 4, *ROW), "pack_own")


def pack_other(scalars, own, other):
    def kernel(s, *refs):
        pack_rows(s, refs[:6], refs[7])

    def spec(a):
        return pl.BlockSpec((None, 2, 64, 256), lambda n, s: (a, 0, 0, n))

    return call(
        kernel, scalars, [other] * 6 + [own], (4,),
        [spec(a) for a in range(6)] + [pl.BlockSpec(memory_space=pl.ANY)],
        pl.BlockSpec((4, 3, 2) + ROW, lambda n, s: (n, 0, 1, 0, 0)),
        out_like(*own.shape), "pack_other", input_output_aliases={7: 0})


def other_heads(scalars, arrays):
    def kernel(s, *refs):
        for a in range(6):
            refs[6][a] = refs[a][...]

    return call(
        kernel, scalars, arrays, (2,),
        [pl.BlockSpec((2, 64, 512), lambda n, s: (0, 0, 2 * (1 - s[0]) + n))] * 6,
        pl.BlockSpec((6, 2, 64, 512), lambda n, s: (0, 0, 0, n)),
        out_like(6, 2, 64, 1024), "other_heads")


def soft_parts(s, ds):
    e = jnp.exp(s - jnp.max(s, axis=-1, keepdims=True))
    p = e * (1.0 / jnp.sum(e, axis=-1, keepdims=True))
    dp = p * (ds - jnp.sum(p * ds, axis=-1, keepdims=True))
    return p.astype(BF16), dp.astype(BF16)


def spatial_kernel(x_ref, out_ref, q_both, q_low, values):
    block = pl.program_id(1)
    count = q_both.shape[0]

    @pl.when(block == 0)
    def _():
        q = x_ref[:, 0, 0].reshape(count, LANES) * BF16(HEAD_DIM ** -0.5)
        v = x_ref[:, 2, 0].reshape(count, LANES)
        q_both[...] = q
        q_low[...] = dot(q, shift_lanes(True)).astype(BF16)
        values[:count] = v
        values[count:] = dot(v, shift_lanes(False)).astype(BF16)

    rows = count // 2
    here = pl.ds(pl.multiple_of(block * rows, rows), rows)
    keys = x_ref[:, 1, 0].reshape(count, LANES)
    s = dot_t(q_low[here, :], keys)
    ds = dot_t(q_both[here, :], keys)
    found = dot(jnp.concatenate(soft_parts(s, ds), axis=-1), values[...]).astype(BF16)
    out_ref[:, 0] = found.reshape(8, 64, LANES)


def spatial(x):
    rows = pltpu.VMEM((1024, LANES), BF16)
    return pl.pallas_call(
        spatial_kernel,
        grid=(4, 2),
        in_specs=[pl.BlockSpec((16, 3, 1) + ROW, lambda f, b: (0, 0, f, 0, 0))],
        out_specs=pl.BlockSpec((8, 1) + ROW, lambda f, b: (b, f, 0, 0)),
        out_shape=out_like(16, 4, *ROW),
        scratch_shapes=[rows, rows, pltpu.VMEM((2048, LANES), BF16)],
        compiler_params=pltpu.CompilerParams(vmem_limit_bytes=VMEM_LIMIT),
        cost_estimate=COST,
        name="spatial",
    )(x)


def temporal_kernel(x_ref, out_ref):
    row = lax.broadcasted_iota(jnp.int32, (256, 256), 0)
    col = lax.broadcasted_iota(jnp.int32, (256, 256), 1)
    turn = jnp.where(col == (row % 16) * 16 + row // 16, 1.0, 0.0).astype(BF16)
    down, up = shift_lanes(True), shift_lanes(False)
    moved = []
    for i in range(4):
        rows = jnp.concatenate([x_ref[4 * i:4 * i + 4, a].reshape(256, LANES) for a in range(3)], axis=-1)
        rows = dot(turn, rows).astype(BF16)
        q, k, v = [rows[:, a * LANES:(a + 1) * LANES] for a in range(3)]
        q = q * BF16(HEAD_DIM ** -0.5)
        moved.append((q, dot(q, down).astype(BF16), k, v, dot(v, up).astype(BF16)))
    row = lax.broadcasted_iota(jnp.int32, (LANES, LANES), 0)
    col = lax.broadcasted_iota(jnp.int32, (LANES, LANES), 1)
    same = (row // 64) == (col // 64)
    pieces = []
    for g in range(8):
        q, q_low, k, v, v_up = [
            jnp.concatenate(
                [moved[i][m][t * 16:(t + 1) * 16] for t in (2 * g, 2 * g + 1) for i in range(4)], axis=0)
            for m in range(5)]
        scores = dot_t(jnp.concatenate([q_low, q], axis=0), k)
        p, dp = soft_parts(jnp.where(same, scores[:LANES], -jnp.inf), scores[LANES:])
        found = dot(jnp.concatenate([p, dp], axis=-1), jnp.concatenate([v, v_up], axis=0))
        pieces.append(found.astype(BF16))
    back = []
    for i in range(4):
        back.append(jnp.concatenate(
            [pieces[t // 2][(t % 2) * 64 + i * 16:(t % 2) * 64 + i * 16 + 16] for t in range(16)], axis=0))
    back = dot(turn, jnp.concatenate(back, axis=-1)).astype(BF16)
    for i in range(4):
        out_ref[4 * i:4 * i + 4] = back[:, i * LANES:(i + 1) * LANES].reshape(4, 4, 16, LANES)


def temporal(x):
    return pl.pallas_call(
        temporal_kernel,
        grid=(4,),
        in_specs=[pl.BlockSpec((16, 3, 4, 16, LANES), lambda t: (0, 0, 0, t, 0))],
        out_specs=pl.BlockSpec((16, 4, 16, LANES), lambda t: (0, 0, t, 0)),
        out_shape=out_like(16, 4, *ROW),
        compiler_params=pltpu.CompilerParams(vmem_limit_bytes=VMEM_LIMIT),
        cost_estimate=COST,
        name="temporal",
    )(x)


def add_round(a, b):
    return (a.astype(F32) + b.astype(F32)).astype(BF16)


def finish(scalars, value, other, after):
    def kernel(s, value_ref, other_ref, after_ref, out_ref, d_out_ref):
        swap = swap_lanes()
        side = pl.program_id(0) // 2
        rows = []
        for pair in range(4):
            halves = []
            for half in range(2):
                d = (2 * pair + half) ^ s[1]
                halves.append(jnp.where(side == 0, value_ref[d].reshape(128, LANES), other_ref[d].reshape(128, LANES)))
            rows.append(jnp.concatenate(halves, axis=-1))
        rows = dot(jnp.concatenate(rows, axis=0), swap).astype(BF16)
        for pair in range(4):
            for i, ref in ((0, out_ref), (1, d_out_ref)):
                ref[:, :, pair * LANES:(pair + 1) * LANES] = (
                    rows[128 * pair:128 * pair + 128, i * LANES:(i + 1) * LANES].reshape(2, 64, LANES))

    block = (8, 2) + ROW
    result = pl.BlockSpec((2, 64, 512), lambda n, s: (0, 0, 2 * ((n // 2) ^ s[0]) + n % 2))
    return call(
        kernel, scalars, [value, other, after], (4,),
        [pl.BlockSpec(block, lambda n, s: (jnp.minimum(n, 1), 0, 0, 0)),
         pl.BlockSpec(block, lambda n, s: (jnp.maximum(n - 2, 0), 0, 0, 0)),
         pl.BlockSpec(memory_space=pl.ANY)],
        [result, result], [out_like(2, 64, 2048)] * 2, "finish")


def body(*arrays):
    arrays = list(arrays)
    time = lax.axis_index("tm")
    core = time % 2
    scalars = jnp.stack([core, 3 * ((time // 2) % 2)]).astype(jnp.int32)
    other = swap_cores(other_heads(scalars, arrays))
    packed = pack_other(scalars, pack_own(scalars, arrays), other)

    def to_space(x):
        return exchange(x, "space")

    tokens = lax.cond(core == 0, to_space, lambda x: x, packed)
    tokens, passed = lax.optimization_barrier((tokens, swap_cores(tokens[0, 0, 0, :16])))
    tokens = lax.cond(core == 1, to_space, lambda x: x, tokens)
    in_space, times = lax.optimization_barrier((spatial(tokens), exchange(tokens, "mirrored")))
    total = add_round(in_space, exchange(temporal(times), "mirrored"))
    total = exchange(total, "space")
    return tuple(finish(scalars, total, swap_cores(total[:, 2:]), passed))


def solution(mesh):
    spec = P("tm", "space", None)
    return jax.shard_map(
        body, mesh=mesh, in_specs=(spec,) * 6, out_specs=(spec,) * 2, check_vma=False)
```

```python
import jax
import jax.numpy as jnp
import numpy as np
from jax import lax
from jax.experimental import pallas as pl
from jax.experimental.pallas import tpu as pltpu
from jax.sharding import PartitionSpec as P

HEAD_DIM = 64
LANES = 128
F32 = jnp.float32
BF16 = jnp.bfloat16
VMEM_LIMIT = 50 * 1024 * 1024
COST = pl.CostEstimate(flops=0, bytes_accessed=1024, transcendentals=0)


def dot_t(a, b):
    return lax.dot_general(a, b, (((1,), (1,)), ((), ())), preferred_element_type=F32)


def dot(a, b):
    return jnp.dot(a, b, preferred_element_type=F32)


MESH = (8, 2, 2, 4, 4)
AXES = ("tm", "space")
ROW = (64, LANES)


def groups_of(kind, core):
    ids = np.arange(512).reshape(MESH)[:, :, core]
    if kind == "space":
        found = [ids[y, zh].reshape(-1) for y in range(8) for zh in range(2)]
    else:
        found = [np.stack([ids[:, 0, x, z], ids[:, 1, x, z ^ 3]], axis=1).reshape(-1)
                 for x in range(4) for z in range(4)]
    return [[int(i) for i in group] for group in found]


def exchange(value, kind):
    return lax.all_to_all(
        value, AXES, split_axis=0, concat_axis=0, tiled=True,
        axis_index_groups=groups_of(kind, 0) + groups_of(kind, 1))


def swap_cores(value):
    ids = np.arange(512).reshape(MESH)
    pairs = zip(ids.reshape(-1), ids[:, :, ::-1].reshape(-1))
    return lax.ppermute(value, AXES, [(int(a), int(b)) for a, b in pairs])


def call(kernel, scalars, operands, grid, in_specs, out_specs, out_shape, name, **kwargs):
    return pl.pallas_call(
        kernel,
        grid_spec=pltpu.PrefetchScalarGridSpec(
            num_scalar_prefetch=1, grid=grid, in_specs=in_specs, out_specs=out_specs),
        out_shape=out_shape,
        cost_estimate=COST,
        name=name,
        **kwargs,
    )(scalars, *operands)


def out_like(*shape):
    return jax.ShapeDtypeStruct(shape, BF16)


def swap_lanes():
    row = lax.broadcasted_iota(jnp.int32, (256, 256), 0)
    col = lax.broadcasted_iota(jnp.int32, (256, 256), 1)
    block = col // 64
    source = jnp.where(block == 1, col + 64, jnp.where(block == 2, col - 64, col))
    return jnp.where(row == source, 1.0, 0.0).astype(BF16)


def shift_lanes(down):
    row = lax.broadcasted_iota(jnp.int32, (LANES, LANES), 0)
    col = lax.broadcasted_iota(jnp.int32, (LANES, LANES), 1)
    return jnp.where(row == col + (64 if down else -64), 1.0, 0.0).astype(BF16)


def pack_rows(s, refs, out):
    swap = swap_lanes()
    rows = [
        jnp.concatenate(
            [refs[m][:, :, pair * LANES:(pair + 1) * LANES].reshape(128, LANES) for m in members], axis=-1)
        for pair in range(2) for members in ((3, 0), (1, 4), (2, 5))]
    rows = dot(jnp.concatenate(rows, axis=0), swap).astype(BF16)
    for pair in range(2):
        for a in range(3):
            for half in range(2):
                out[(2 * pair + half) ^ s[1], a] = (
                    rows[(3 * pair + a) * 128:(3 * pair + a + 1) * 128, half * LANES:(half + 1) * LANES]
                    .reshape(2, 64, LANES))


def pack_own(scalars, arrays):
    def kernel(s, *refs):
        pack_rows(s, refs[:6], refs[6])

    return call(
        kernel, scalars, arrays, (4,),
        [pl.BlockSpec((2, 64, 256), lambda n, s: (0, 0, 4 * s[0] + n))] * 6,
        pl.BlockSpec((4, 3, 2) + ROW, lambda n, s: (n, 0, 0, 0, 0)),
        out_like(16, 3, 4, *ROW), "pack_own")


def pack_other(scalars, own, other):
    def kernel(s, *refs):
        pack_rows(s, refs[:6], refs[7])

    def spec(a):
        return pl.BlockSpec((None, 2, 64, 256), lambda n, s: (a, 0, 0, n))

    return call(
        kernel, scalars, [other] * 6 + [own], (4,),
        [spec(a) for a in range(6)] + [pl.BlockSpec(memory_space=pl.ANY)],
        pl.BlockSpec((4, 3, 2) + ROW, lambda n, s: (n, 0, 1, 0, 0)),
        out_like(*own.shape), "pack_other", input_output_aliases={7: 0})


def other_heads(scalars, arrays):
    def kernel(s, *refs):
        for a in range(6):
            refs[6][a] = refs[a][...]

    return call(
        kernel, scalars, arrays, (2,),
        [pl.BlockSpec((2, 64, 512), lambda n, s: (0, 0, 2 * (1 - s[0]) + n))] * 6,
        pl.BlockSpec((6, 2, 64, 512), lambda n, s: (0, 0, 0, n)),
        out_like(6, 2, 64, 1024), "other_heads")


def soft_parts(s, ds):
    e = jnp.exp(s - jnp.max(s, axis=-1, keepdims=True))
    p = e * (1.0 / jnp.sum(e, axis=-1, keepdims=True))
    dp = p * (ds - jnp.sum(p * ds, axis=-1, keepdims=True))
    return p.astype(BF16), dp.astype(BF16)


def spatial_kernel(x_ref, out_ref):
    q, keys, v = [x_ref[:, a, 0].reshape(1024, LANES) for a in range(3)]
    q = q * BF16(HEAD_DIM ** -0.5)
    q_low = dot(q, shift_lanes(True)).astype(BF16)
    values = jnp.concatenate([v, dot(v, shift_lanes(False)).astype(BF16)], axis=0)
    for block in range(2):
        rows = slice(512 * block, 512 * block + 512)
        both = jnp.concatenate(soft_parts(dot_t(q_low[rows], keys), dot_t(q[rows], keys)), axis=-1)
        out_ref[8 * block:8 * block + 8, 0] = dot(both, values).astype(BF16).reshape(8, 64, LANES)


def spatial(x):
    return pl.pallas_call(
        spatial_kernel,
        grid=(4,),
        in_specs=[pl.BlockSpec((16, 3, 1) + ROW, lambda f: (0, 0, f, 0, 0))],
        out_specs=pl.BlockSpec((16, 1) + ROW, lambda f: (0, f, 0, 0)),
        out_shape=out_like(16, 4, *ROW),
        compiler_params=pltpu.CompilerParams(vmem_limit_bytes=VMEM_LIMIT),
        cost_estimate=COST,
        name="spatial",
    )(x)


def temporal_kernel(x_ref, out_ref):
    row = lax.broadcasted_iota(jnp.int32, (256, 256), 0)
    col = lax.broadcasted_iota(jnp.int32, (256, 256), 1)
    turn = jnp.where(col == (row % 16) * 16 + row // 16, 1.0, 0.0).astype(BF16)
    down, up = shift_lanes(True), shift_lanes(False)
    moved = []
    for i in range(4):
        rows = jnp.concatenate([x_ref[4 * i:4 * i + 4, a].reshape(256, LANES) for a in range(3)], axis=-1)
        rows = dot(turn, rows).astype(BF16)
        q, k, v = [rows[:, a * LANES:(a + 1) * LANES] for a in range(3)]
        q = q * BF16(HEAD_DIM ** -0.5)
        moved.append((q, dot(q, down).astype(BF16), k, v, dot(v, up).astype(BF16)))
    row = lax.broadcasted_iota(jnp.int32, (LANES, LANES), 0)
    col = lax.broadcasted_iota(jnp.int32, (LANES, LANES), 1)
    same = (row // 64) == (col // 64)
    pieces = []
    for g in range(8):
        q, q_low, k, v, v_up = [
            jnp.concatenate(
                [moved[i][m][t * 16:(t + 1) * 16] for t in (2 * g, 2 * g + 1) for i in range(4)], axis=0)
            for m in range(5)]
        scores = dot_t(jnp.concatenate([q_low, q], axis=0), k)
        p, dp = soft_parts(jnp.where(same, scores[:LANES], -jnp.inf), scores[LANES:])
        found = dot(jnp.concatenate([p, dp], axis=-1), jnp.concatenate([v, v_up], axis=0))
        pieces.append(found.astype(BF16))
    back = []
    for i in range(4):
        back.append(jnp.concatenate(
            [pieces[t // 2][(t % 2) * 64 + i * 16:(t % 2) * 64 + i * 16 + 16] for t in range(16)], axis=0))
    back = dot(turn, jnp.concatenate(back, axis=-1)).astype(BF16)
    for i in range(4):
        out_ref[4 * i:4 * i + 4] = back[:, i * LANES:(i + 1) * LANES].reshape(4, 4, 16, LANES)


def temporal(x):
    return pl.pallas_call(
        temporal_kernel,
        grid=(4,),
        in_specs=[pl.BlockSpec((16, 3, 4, 16, LANES), lambda t: (0, 0, 0, t, 0))],
        out_specs=pl.BlockSpec((16, 4, 16, LANES), lambda t: (0, 0, t, 0)),
        out_shape=out_like(16, 4, *ROW),
        compiler_params=pltpu.CompilerParams(vmem_limit_bytes=VMEM_LIMIT),
        cost_estimate=COST,
        name="temporal",
    )(x)


def add_round(a, b):
    return (a.astype(F32) + b.astype(F32)).astype(BF16)


def finish(scalars, value, other, after):
    def kernel(s, value_ref, other_ref, after_ref, out_ref, d_out_ref):
        swap = swap_lanes()
        side = pl.program_id(0) // 2
        rows = []
        for pair in range(4):
            halves = []
            for half in range(2):
                d = (2 * pair + half) ^ s[1]
                halves.append(jnp.where(side == 0, value_ref[d].reshape(128, LANES), other_ref[d].reshape(128, LANES)))
            rows.append(jnp.concatenate(halves, axis=-1))
        rows = dot(jnp.concatenate(rows, axis=0), swap).astype(BF16)
        for pair in range(4):
            for i, ref in ((0, out_ref), (1, d_out_ref)):
                ref[:, :, pair * LANES:(pair + 1) * LANES] = (
                    rows[128 * pair:128 * pair + 128, i * LANES:(i + 1) * LANES].reshape(2, 64, LANES))

    block = (8, 2) + ROW
    result = pl.BlockSpec((2, 64, 512), lambda n, s: (0, 0, 2 * ((n // 2) ^ s[0]) + n % 2))
    return call(
        kernel, scalars, [value, other, after], (4,),
        [pl.BlockSpec(block, lambda n, s: (jnp.minimum(n, 1), 0, 0, 0)),
         pl.BlockSpec(block, lambda n, s: (jnp.maximum(n - 2, 0), 0, 0, 0)),
         pl.BlockSpec(memory_space=pl.ANY)],
        [result, result], [out_like(2, 64, 2048)] * 2, "finish")


def body(*arrays):
    arrays = list(arrays)
    time = lax.axis_index("tm")
    core = time % 2
    scalars = jnp.stack([core, 3 * ((time // 2) % 2)]).astype(jnp.int32)
    other = swap_cores(other_heads(scalars, arrays))
    packed = pack_other(scalars, pack_own(scalars, arrays), other)

    def to_space(x):
        return exchange(x, "space")

    tokens = lax.cond(core == 0, to_space, lambda x: x, packed)
    tokens, passed = lax.optimization_barrier((tokens, swap_cores(tokens[0, 0, 0, :16])))
    tokens = lax.cond(core == 1, to_space, lambda x: x, tokens)
    in_time = temporal(exchange(tokens, "mirrored"))
    total = add_round(spatial(tokens), exchange(in_time, "mirrored"))
    total = exchange(total, "space")
    return tuple(finish(scalars, total, swap_cores(total[:, 2:]), passed))


def solution(mesh):
    spec = P("tm", "space", None)
    return jax.shard_map(
        body, mesh=mesh, in_specs=(spec,) * 6, out_specs=(spec,) * 2, check_vma=False)
```

```python
import jax
import jax.numpy as jnp
import numpy as np
from jax import lax
from jax.experimental import pallas as pl
from jax.experimental.pallas import tpu as pltpu
from jax.sharding import PartitionSpec as P

HEAD_DIM = 64
LANES = 128
F32 = jnp.float32
BF16 = jnp.bfloat16
VMEM_LIMIT = 50 * 1024 * 1024
COST = pl.CostEstimate(flops=0, bytes_accessed=1024, transcendentals=0)


def dot_t(a, b):
    return lax.dot_general(a, b, (((1,), (1,)), ((), ())), preferred_element_type=F32)


def dot(a, b):
    return jnp.dot(a, b, preferred_element_type=F32)


MESH = (8, 2, 2, 4, 4)
AXES = ("tm", "space")
ROW = (64, LANES)


def groups_of(kind, core):
    ids = np.arange(512).reshape(MESH)[:, :, core]
    if kind == "space":
        found = [ids[y, zh].reshape(-1) for y in range(8) for zh in range(2)]
    elif kind == "time":
        found = [ids[:, :, x, z].reshape(-1) for x in range(4) for z in range(4)]
    else:
        found = [np.stack([ids[:, 0, x, z], ids[:, 1, x, z ^ 3]], axis=1).reshape(-1)
                 for x in range(4) for z in range(4)]
    return [[int(i) for i in group] for group in found]


def exchange(value, kind):
    return lax.all_to_all(
        value, AXES, split_axis=0, concat_axis=0, tiled=True,
        axis_index_groups=groups_of(kind, 0) + groups_of(kind, 1))


def swap_cores(value):
    ids = np.arange(512).reshape(MESH)
    pairs = zip(ids.reshape(-1), ids[:, :, ::-1].reshape(-1))
    return lax.ppermute(value, AXES, [(int(a), int(b)) for a, b in pairs])


def call(kernel, scalars, operands, grid, in_specs, out_specs, out_shape, name, **kwargs):
    return pl.pallas_call(
        kernel,
        grid_spec=pltpu.PrefetchScalarGridSpec(
            num_scalar_prefetch=1, grid=grid, in_specs=in_specs, out_specs=out_specs),
        out_shape=out_shape,
        cost_estimate=COST,
        name=name,
        **kwargs,
    )(scalars, *operands)


def out_like(*shape):
    return jax.ShapeDtypeStruct(shape, BF16)


def swap_lanes():
    row = lax.broadcasted_iota(jnp.int32, (256, 256), 0)
    col = lax.broadcasted_iota(jnp.int32, (256, 256), 1)
    block = col // 64
    source = jnp.where(block == 1, col + 64, jnp.where(block == 2, col - 64, col))
    return jnp.where(row == source, 1.0, 0.0).astype(BF16)


def shift_lanes(down):
    row = lax.broadcasted_iota(jnp.int32, (LANES, LANES), 0)
    col = lax.broadcasted_iota(jnp.int32, (LANES, LANES), 1)
    return jnp.where(row == col + (64 if down else -64), 1.0, 0.0).astype(BF16)


def pack_rows(s, refs, out):
    swap = swap_lanes()
    rows = [
        jnp.concatenate(
            [refs[m][:, :, pair * LANES:(pair + 1) * LANES].reshape(128, LANES) for m in members], axis=-1)
        for pair in range(2) for members in ((3, 0), (1, 4), (2, 5))]
    rows = dot(jnp.concatenate(rows, axis=0), swap).astype(BF16)
    for pair in range(2):
        for a in range(3):
            for half in range(2):
                out[(2 * pair + half) ^ s[1], a] = (
                    rows[(3 * pair + a) * 128:(3 * pair + a + 1) * 128, half * LANES:(half + 1) * LANES]
                    .reshape(2, 64, LANES))


def pack_own(scalars, arrays):
    def kernel(s, *refs):
        pack_rows(s, refs[:6], refs[6])

    return call(
        kernel, scalars, arrays, (4,),
        [pl.BlockSpec((2, 64, 256), lambda n, s: (0, 0, 4 * s[0] + n))] * 6,
        pl.BlockSpec((4, 3, 2) + ROW, lambda n, s: (n, 0, 0, 0, 0)),
        out_like(16, 3, 4, *ROW), "pack_own")


def pack_other(scalars, own, other):
    def kernel(s, *refs):
        pack_rows(s, refs[:6], refs[7])

    def spec(a):
        return pl.BlockSpec((None, 2, 64, 256), lambda n, s: (a, 0, 0, n))

    return call(
        kernel, scalars, [other] * 6 + [own], (4,),
        [spec(a) for a in range(6)] + [pl.BlockSpec(memory_space=pl.ANY)],
        pl.BlockSpec((4, 3, 2) + ROW, lambda n, s: (n, 0, 1, 0, 0)),
        out_like(*own.shape), "pack_other", input_output_aliases={7: 0})


def other_heads(scalars, arrays):
    def kernel(s, *refs):
        for a in range(6):
            refs[6][a] = refs[a][...]

    return call(
        kernel, scalars, arrays, (2,),
        [pl.BlockSpec((2, 64, 512), lambda n, s: (0, 0, 2 * (1 - s[0]) + n))] * 6,
        pl.BlockSpec((6, 2, 64, 512), lambda n, s: (0, 0, 0, n)),
        out_like(6, 2, 64, 1024), "other_heads")


def soft_parts(s, ds):
    e = jnp.exp(s - jnp.max(s, axis=-1, keepdims=True))
    p = e * (1.0 / jnp.sum(e, axis=-1, keepdims=True))
    dp = p * (ds - jnp.sum(p * ds, axis=-1, keepdims=True))
    return p.astype(BF16), dp.astype(BF16)


def spatial_kernel(x_ref, out_ref):
    q, keys, v = [x_ref[:, a, 0].reshape(1024, LANES) for a in range(3)]
    q = q * BF16(HEAD_DIM ** -0.5)
    q_low = dot(q, shift_lanes(True)).astype(BF16)
    values = jnp.concatenate([v, dot(v, shift_lanes(False)).astype(BF16)], axis=0)
    for block in range(2):
        rows = slice(512 * block, 512 * block + 512)
        both = jnp.concatenate(soft_parts(dot_t(q_low[rows], keys), dot_t(q[rows], keys)), axis=-1)
        out_ref[8 * block:8 * block + 8, 0] = dot(both, values).astype(BF16).reshape(8, 64, LANES)


def spatial(x):
    return pl.pallas_call(
        spatial_kernel,
        grid=(4,),
        in_specs=[pl.BlockSpec((16, 3, 1) + ROW, lambda f: (0, 0, f, 0, 0))],
        out_specs=pl.BlockSpec((16, 1) + ROW, lambda f: (0, f, 0, 0)),
        out_shape=out_like(16, 4, *ROW),
        compiler_params=pltpu.CompilerParams(vmem_limit_bytes=VMEM_LIMIT),
        cost_estimate=COST,
        name="spatial",
    )(x)


def temporal_kernel(x_ref, out_ref):
    row = lax.broadcasted_iota(jnp.int32, (256, 256), 0)
    col = lax.broadcasted_iota(jnp.int32, (256, 256), 1)
    turn = jnp.where(col == (row % 16) * 16 + row // 16, 1.0, 0.0).astype(BF16)
    down, up = shift_lanes(True), shift_lanes(False)
    moved = []
    for i in range(4):
        rows = jnp.concatenate([x_ref[4 * i:4 * i + 4, a].reshape(256, LANES) for a in range(3)], axis=-1)
        rows = dot(turn, rows).astype(BF16)
        q, k, v = [rows[:, a * LANES:(a + 1) * LANES] for a in range(3)]
        q = q * BF16(HEAD_DIM ** -0.5)
        moved.append((q, dot(q, down).astype(BF16), k, v, dot(v, up).astype(BF16)))
    row = lax.broadcasted_iota(jnp.int32, (LANES, LANES), 0)
    col = lax.broadcasted_iota(jnp.int32, (LANES, LANES), 1)
    same = (row // 64) == (col // 64)
    pieces = []
    for g in range(8):
        q, q_low, k, v, v_up = [
            jnp.concatenate(
                [moved[i][m][t * 16:(t + 1) * 16] for t in (2 * g, 2 * g + 1) for i in range(4)], axis=0)
            for m in range(5)]
        scores = dot_t(jnp.concatenate([q_low, q], axis=0), k)
        p, dp = soft_parts(jnp.where(same, scores[:LANES], -jnp.inf), scores[LANES:])
        found = dot(jnp.concatenate([p, dp], axis=-1), jnp.concatenate([v, v_up], axis=0))
        pieces.append(found.astype(BF16))
    back = []
    for i in range(4):
        back.append(jnp.concatenate(
            [pieces[t // 2][(t % 2) * 64 + i * 16:(t % 2) * 64 + i * 16 + 16] for t in range(16)], axis=0))
    back = dot(turn, jnp.concatenate(back, axis=-1)).astype(BF16)
    for i in range(4):
        out_ref[4 * i:4 * i + 4] = back[:, i * LANES:(i + 1) * LANES].reshape(4, 4, 16, LANES)


def temporal(x):
    return pl.pallas_call(
        temporal_kernel,
        grid=(4,),
        in_specs=[pl.BlockSpec((16, 3, 4, 16, LANES), lambda t: (0, 0, 0, t, 0))],
        out_specs=pl.BlockSpec((16, 4, 16, LANES), lambda t: (0, 0, t, 0)),
        out_shape=out_like(16, 4, *ROW),
        compiler_params=pltpu.CompilerParams(vmem_limit_bytes=VMEM_LIMIT),
        cost_estimate=COST,
        name="temporal",
    )(x)


def add_round(a, b):
    return (a.astype(F32) + b.astype(F32)).astype(BF16)


def finish(scalars, value, other, after):
    def kernel(s, value_ref, other_ref, after_ref, out_ref, d_out_ref):
        swap = swap_lanes()
        side = pl.program_id(0) // 2
        flip = jnp.where(side == 0, s[1], s[2])
        rows = []
        for pair in range(4):
            halves = []
            for half in range(2):
                d = (2 * pair + half) ^ flip
                halves.append(jnp.where(side == 0, value_ref[d].reshape(128, LANES), other_ref[d].reshape(128, LANES)))
            rows.append(jnp.concatenate(halves, axis=-1))
        rows = dot(jnp.concatenate(rows, axis=0), swap).astype(BF16)
        for pair in range(4):
            for i, ref in ((0, out_ref), (1, d_out_ref)):
                ref[:, :, pair * LANES:(pair + 1) * LANES] = (
                    rows[128 * pair:128 * pair + 128, i * LANES:(i + 1) * LANES].reshape(2, 64, LANES))

    block = (8, 2) + ROW
    result = pl.BlockSpec((2, 64, 512), lambda n, s: (0, 0, 2 * ((n // 2) ^ s[0]) + n % 2))
    return call(
        kernel, scalars, [value, other, after], (4,),
        [pl.BlockSpec(block, lambda n, s: (jnp.minimum(n, 1), 0, 0, 0)),
         pl.BlockSpec(block, lambda n, s: (jnp.maximum(n - 2, 0), 0, 0, 0)),
         pl.BlockSpec(memory_space=pl.ANY)],
        [result, result], [out_like(2, 64, 2048)] * 2, "finish")


def body(*arrays):
    arrays = list(arrays)
    time = lax.axis_index("tm")
    core, zh3 = time % 2, 3 * ((time // 2) % 2)
    scalars = jnp.stack([core, zh3 * (1 - core), zh3 * core]).astype(jnp.int32)
    other = swap_cores(other_heads(scalars, arrays))
    packed = pack_other(scalars, pack_own(scalars, arrays), other)

    def lead(x):
        return exchange(x, "space"), jnp.zeros((16, 4) + ROW, BF16)

    def follow(x):
        return x, temporal(exchange(x, "time"))

    def lead_rest(x, _):
        found = exchange(temporal(exchange(x, "mirrored")), "mirrored")
        return exchange(add_round(spatial(x), found), "space")

    def follow_rest(x, in_time):
        x = exchange(x, "space")
        found = exchange(in_time, "time")
        return add_round(exchange(spatial(x), "space"), found)

    tokens, in_time = lax.cond(core == 0, lead, follow, packed)
    tokens, passed = lax.optimization_barrier((tokens, swap_cores(tokens[0, 0, 0, :16])))
    total = lax.cond(core == 0, lead_rest, follow_rest, tokens, in_time)
    return tuple(finish(scalars, total, swap_cores(total[:, 2:]), passed))


def solution(mesh):
    spec = P("tm", "space", None)
    return jax.shard_map(
        body, mesh=mesh, in_specs=(spec,) * 6, out_specs=(spec,) * 2, check_vma=False)
```

```python
import jax
import jax.numpy as jnp
import numpy as np
from jax import lax
from jax.experimental import pallas as pl
from jax.experimental.pallas import tpu as pltpu
from jax.sharding import PartitionSpec as P

HEAD_DIM = 64
LANES = 128
F32 = jnp.float32
BF16 = jnp.bfloat16
VMEM_LIMIT = 50 * 1024 * 1024
COST = pl.CostEstimate(flops=0, bytes_accessed=1024, transcendentals=0)


def dot_t(a, b):
    return lax.dot_general(a, b, (((1,), (1,)), ((), ())), preferred_element_type=F32)


def dot(a, b):
    return jnp.dot(a, b, preferred_element_type=F32)


MESH = (8, 2, 2, 4, 4)
AXES = ("tm", "space")
ROW = (64, LANES)


def groups_of(kind, core):
    ids = np.arange(512).reshape(MESH)[:, :, core]
    if kind == "space":
        found = [ids[y, zh].reshape(-1) for y in range(8) for zh in range(2)]
    elif kind == "time":
        found = [ids[:, :, x, z].reshape(-1) for x in range(4) for z in range(4)]
    else:
        found = [np.stack([ids[:, 0, x, z], ids[:, 1, x, z ^ 3]], axis=1).reshape(-1)
                 for x in range(4) for z in range(4)]
    return [[int(i) for i in group] for group in found]


def exchange(value, kind):
    return lax.all_to_all(
        value, AXES, split_axis=0, concat_axis=0, tiled=True,
        axis_index_groups=groups_of(kind, 0) + groups_of(kind, 1))


def swap_cores(value):
    ids = np.arange(512).reshape(MESH)
    pairs = zip(ids.reshape(-1), ids[:, :, ::-1].reshape(-1))
    return lax.ppermute(value, AXES, [(int(a), int(b)) for a, b in pairs])


def call(kernel, scalars, operands, grid, in_specs, out_specs, out_shape, name, **kwargs):
    return pl.pallas_call(
        kernel,
        grid_spec=pltpu.PrefetchScalarGridSpec(
            num_scalar_prefetch=1, grid=grid, in_specs=in_specs, out_specs=out_specs),
        out_shape=out_shape,
        cost_estimate=COST,
        name=name,
        **kwargs,
    )(scalars, *operands)


def out_like(*shape):
    return jax.ShapeDtypeStruct(shape, BF16)


def swap_lanes():
    row = lax.broadcasted_iota(jnp.int32, (256, 256), 0)
    col = lax.broadcasted_iota(jnp.int32, (256, 256), 1)
    block = col // 64
    source = jnp.where(block == 1, col + 64, jnp.where(block == 2, col - 64, col))
    return jnp.where(row == source, 1.0, 0.0).astype(BF16)


def shift_lanes(down):
    row = lax.broadcasted_iota(jnp.int32, (LANES, LANES), 0)
    col = lax.broadcasted_iota(jnp.int32, (LANES, LANES), 1)
    return jnp.where(row == col + (64 if down else -64), 1.0, 0.0).astype(BF16)


def pack_rows(s, refs, out):
    swap = swap_lanes()
    rows = [
        jnp.concatenate(
            [refs[m][:, :, pair * LANES:(pair + 1) * LANES].reshape(128, LANES) for m in members], axis=-1)
        for pair in range(2) for members in ((3, 0), (1, 4), (2, 5))]
    rows = dot(jnp.concatenate(rows, axis=0), swap).astype(BF16)
    for pair in range(2):
        for a in range(3):
            for half in range(2):
                out[(2 * pair + half) ^ s[1], a] = (
                    rows[(3 * pair + a) * 128:(3 * pair + a + 1) * 128, half * LANES:(half + 1) * LANES]
                    .reshape(2, 64, LANES))


def pack_own(scalars, arrays):
    def kernel(s, *refs):
        pack_rows(s, refs[:6], refs[6])

    return call(
        kernel, scalars, arrays, (4,),
        [pl.BlockSpec((2, 64, 256), lambda n, s: (0, 0, 4 * s[0] + n))] * 6,
        pl.BlockSpec((4, 3, 2) + ROW, lambda n, s: (n, 0, 0, 0, 0)),
        out_like(16, 3, 4, *ROW), "pack_own")


def pack_other(scalars, own, other):
    def kernel(s, *refs):
        pack_rows(s, refs[:6], refs[7])

    def spec(a):
        return pl.BlockSpec((None, 2, 64, 256), lambda n, s: (a, 0, 0, n))

    return call(
        kernel, scalars, [other] * 6 + [own], (4,),
        [spec(a) for a in range(6)] + [pl.BlockSpec(memory_space=pl.ANY)],
        pl.BlockSpec((4, 3, 2) + ROW, lambda n, s: (n, 0, 1, 0, 0)),
        out_like(*own.shape), "pack_other", input_output_aliases={7: 0})


def other_heads(scalars, arrays):
    def kernel(s, *refs):
        for a in range(6):
            refs[6][a] = refs[a][...]

    return call(
        kernel, scalars, arrays, (2,),
        [pl.BlockSpec((2, 64, 512), lambda n, s: (0, 0, 2 * (1 - s[0]) + n))] * 6,
        pl.BlockSpec((6, 2, 64, 512), lambda n, s: (0, 0, 0, n)),
        out_like(6, 2, 64, 1024), "other_heads")


def soft_parts(s, ds):
    e = jnp.exp(s - jnp.max(s, axis=-1, keepdims=True))
    p = e * (1.0 / jnp.sum(e, axis=-1, keepdims=True))
    dp = p * (ds - jnp.sum(p * ds, axis=-1, keepdims=True))
    return p.astype(BF16), dp.astype(BF16)


def spatial_kernel(x_ref, out_ref):
    q, keys, v = [x_ref[:, a, 0].reshape(1024, LANES) for a in range(3)]
    q = q * BF16(HEAD_DIM ** -0.5)
    q_low = dot(q, shift_lanes(True)).astype(BF16)
    values = jnp.concatenate([v, dot(v, shift_lanes(False)).astype(BF16)], axis=0)
    for block in range(2):
        rows = slice(512 * block, 512 * block + 512)
        both = jnp.concatenate(soft_parts(dot_t(q_low[rows], keys), dot_t(q[rows], keys)), axis=-1)
        out_ref[8 * block:8 * block + 8, 0] = dot(both, values).astype(BF16).reshape(8, 64, LANES)


def spatial(x):
    return pl.pallas_call(
        spatial_kernel,
        grid=(4,),
        in_specs=[pl.BlockSpec((16, 3, 1) + ROW, lambda f: (0, 0, f, 0, 0))],
        out_specs=pl.BlockSpec((16, 1) + ROW, lambda f: (0, f, 0, 0)),
        out_shape=out_like(16, 4, *ROW),
        compiler_params=pltpu.CompilerParams(vmem_limit_bytes=VMEM_LIMIT),
        cost_estimate=COST,
        name="spatial",
    )(x)


def temporal_kernel(x_ref, out_ref):
    row = lax.broadcasted_iota(jnp.int32, (256, 256), 0)
    col = lax.broadcasted_iota(jnp.int32, (256, 256), 1)
    turn = jnp.where(col == (row % 16) * 16 + row // 16, 1.0, 0.0).astype(BF16)
    down, up = shift_lanes(True), shift_lanes(False)
    moved = []
    for i in range(4):
        rows = jnp.concatenate([x_ref[4 * i:4 * i + 4, a].reshape(256, LANES) for a in range(3)], axis=-1)
        rows = dot(turn, rows).astype(BF16)
        q, k, v = [rows[:, a * LANES:(a + 1) * LANES] for a in range(3)]
        q = q * BF16(HEAD_DIM ** -0.5)
        moved.append((q, dot(q, down).astype(BF16), k, v, dot(v, up).astype(BF16)))
    row = lax.broadcasted_iota(jnp.int32, (LANES, LANES), 0)
    col = lax.broadcasted_iota(jnp.int32, (LANES, LANES), 1)
    same = (row // 64) == (col // 64)
    pieces = []
    for g in range(8):
        q, q_low, k, v, v_up = [
            jnp.concatenate(
                [moved[i][m][t * 16:(t + 1) * 16] for t in (2 * g, 2 * g + 1) for i in range(4)], axis=0)
            for m in range(5)]
        scores = dot_t(jnp.concatenate([q_low, q], axis=0), k)
        p, dp = soft_parts(jnp.where(same, scores[:LANES], -jnp.inf), scores[LANES:])
        found = dot(jnp.concatenate([p, dp], axis=-1), jnp.concatenate([v, v_up], axis=0))
        pieces.append(found.astype(BF16))
    back = []
    for i in range(4):
        back.append(jnp.concatenate(
            [pieces[t // 2][(t % 2) * 64 + i * 16:(t % 2) * 64 + i * 16 + 16] for t in range(16)], axis=0))
    back = dot(turn, jnp.concatenate(back, axis=-1)).astype(BF16)
    for i in range(4):
        out_ref[4 * i:4 * i + 4] = back[:, i * LANES:(i + 1) * LANES].reshape(4, 4, 16, LANES)


def temporal(x):
    return pl.pallas_call(
        temporal_kernel,
        grid=(4,),
        in_specs=[pl.BlockSpec((16, 3, 4, 16, LANES), lambda t: (0, 0, 0, t, 0))],
        out_specs=pl.BlockSpec((16, 4, 16, LANES), lambda t: (0, 0, t, 0)),
        out_shape=out_like(16, 4, *ROW),
        compiler_params=pltpu.CompilerParams(vmem_limit_bytes=VMEM_LIMIT),
        cost_estimate=COST,
        name="temporal",
    )(x)


def add_round(a, b):
    return (a.astype(F32) + b.astype(F32)).astype(BF16)


def finish(scalars, value, other, after):
    def kernel(s, value_ref, other_ref, after_ref, out_ref, d_out_ref):
        swap = swap_lanes()
        side = pl.program_id(0) // 2
        flip = jnp.where(side == 0, s[1], s[2])
        rows = []
        for pair in range(4):
            halves = []
            for half in range(2):
                d = (2 * pair + half) ^ flip
                halves.append(jnp.where(side == 0, value_ref[d].reshape(128, LANES), other_ref[d].reshape(128, LANES)))
            rows.append(jnp.concatenate(halves, axis=-1))
        rows = dot(jnp.concatenate(rows, axis=0), swap).astype(BF16)
        for pair in range(4):
            for i, ref in ((0, out_ref), (1, d_out_ref)):
                ref[:, :, pair * LANES:(pair + 1) * LANES] = (
                    rows[128 * pair:128 * pair + 128, i * LANES:(i + 1) * LANES].reshape(2, 64, LANES))

    block = (8, 2) + ROW
    result = pl.BlockSpec((2, 64, 512), lambda n, s: (0, 0, 2 * ((n // 2) ^ s[0]) + n % 2))
    return call(
        kernel, scalars, [value, other, after], (4,),
        [pl.BlockSpec(block, lambda n, s: (jnp.minimum(n, 1), 0, 0, 0)),
         pl.BlockSpec(block, lambda n, s: (jnp.maximum(n - 2, 0), 0, 0, 0)),
         pl.BlockSpec(memory_space=pl.ANY)],
        [result, result], [out_like(2, 64, 2048)] * 2, "finish")


def body(*arrays):
    arrays = list(arrays)
    time = lax.axis_index("tm")
    core, zh3 = time % 2, 3 * ((time // 2) % 2)
    scalars = jnp.stack([core, zh3 * (1 - core), zh3 * core]).astype(jnp.int32)
    other = swap_cores(other_heads(scalars, arrays))
    packed = pack_other(scalars, pack_own(scalars, arrays), other)

    def lead(x):
        return exchange(x, "space"), jnp.zeros((16, 4) + ROW, BF16)

    def follow(x):
        return x, exchange(temporal(exchange(x, "time")), "time")

    def lead_rest(x, _):
        found = exchange(temporal(exchange(x, "mirrored")), "mirrored")
        return exchange(add_round(spatial(x), found), "space")

    def follow_rest(x, found):
        return add_round(exchange(spatial(exchange(x, "space")), "space"), found)

    tokens, found = lax.cond(core == 0, lead, follow, packed)
    tokens, passed = lax.optimization_barrier((tokens, swap_cores(tokens[0, 0, 0, :16])))
    total = lax.cond(core == 0, lead_rest, follow_rest, tokens, found)
    return tuple(finish(scalars, total, swap_cores(total[:, 2:]), passed))


def solution(mesh):
    spec = P("tm", "space", None)
    return jax.shard_map(
        body, mesh=mesh, in_specs=(spec,) * 6, out_specs=(spec,) * 2, check_vma=False)
```

```python
import jax
import jax.numpy as jnp
import numpy as np
from jax import lax
from jax.experimental import pallas as pl
from jax.experimental.pallas import tpu as pltpu
from jax.sharding import PartitionSpec as P

HEAD_DIM = 64
LANES = 128
F32 = jnp.float32
BF16 = jnp.bfloat16
VMEM_LIMIT = 50 * 1024 * 1024
COST = pl.CostEstimate(flops=0, bytes_accessed=1024, transcendentals=0)


def dot_t(a, b):
    return lax.dot_general(a, b, (((1,), (1,)), ((), ())), preferred_element_type=F32)


def dot(a, b):
    return jnp.dot(a, b, preferred_element_type=F32)


MESH = (8, 2, 2, 4, 4)
AXES = ("tm", "space")
ROW = (64, LANES)


def groups_of(kind, core):
    ids = np.arange(512).reshape(MESH)[:, :, core]
    if kind == "space":
        found = [ids[y, zh].reshape(-1) for y in range(8) for zh in range(2)]
    elif kind == "time":
        found = [ids[:, :, x, z].reshape(-1) for x in range(4) for z in range(4)]
    else:
        found = [np.stack([ids[:, 0, x, z], ids[:, 1, x, z ^ 3]], axis=1).reshape(-1)
                 for x in range(4) for z in range(4)]
    return [[int(i) for i in group] for group in found]


def exchange(value, kind):
    return lax.all_to_all(
        value, AXES, split_axis=0, concat_axis=0, tiled=True,
        axis_index_groups=groups_of(kind, 0) + groups_of(kind, 1))


def swap_cores(value):
    ids = np.arange(512).reshape(MESH)
    pairs = zip(ids.reshape(-1), ids[:, :, ::-1].reshape(-1))
    return lax.ppermute(value, AXES, [(int(a), int(b)) for a, b in pairs])


def call(kernel, scalars, operands, grid, in_specs, out_specs, out_shape, name, **kwargs):
    return pl.pallas_call(
        kernel,
        grid_spec=pltpu.PrefetchScalarGridSpec(
            num_scalar_prefetch=1, grid=grid, in_specs=in_specs, out_specs=out_specs),
        out_shape=out_shape,
        cost_estimate=COST,
        name=name,
        **kwargs,
    )(scalars, *operands)


def out_like(*shape):
    return jax.ShapeDtypeStruct(shape, BF16)


def swap_lanes():
    row = lax.broadcasted_iota(jnp.int32, (256, 256), 0)
    col = lax.broadcasted_iota(jnp.int32, (256, 256), 1)
    block = col // 64
    source = jnp.where(block == 1, col + 64, jnp.where(block == 2, col - 64, col))
    return jnp.where(row == source, 1.0, 0.0).astype(BF16)


def shift_lanes(down):
    row = lax.broadcasted_iota(jnp.int32, (LANES, LANES), 0)
    col = lax.broadcasted_iota(jnp.int32, (LANES, LANES), 1)
    return jnp.where(row == col + (64 if down else -64), 1.0, 0.0).astype(BF16)


def pack_rows(s, refs, out):
    swap = swap_lanes()
    rows = [
        jnp.concatenate(
            [refs[m][:, :, pair * LANES:(pair + 1) * LANES].reshape(128, LANES) for m in members], axis=-1)
        for pair in range(2) for members in ((3, 0), (1, 4), (2, 5))]
    rows = dot(jnp.concatenate(rows, axis=0), swap).astype(BF16)
    for pair in range(2):
        for a in range(3):
            for half in range(2):
                out[(2 * pair + half) ^ s[1], a] = (
                    rows[(3 * pair + a) * 128:(3 * pair + a + 1) * 128, half * LANES:(half + 1) * LANES]
                    .reshape(2, 64, LANES))


def pack_own(scalars, arrays):
    def kernel(s, *refs):
        pack_rows(s, refs[:6], refs[6])

    return call(
        kernel, scalars, arrays, (4,),
        [pl.BlockSpec((2, 64, 256), lambda n, s: (0, 0, 4 * s[0] + n))] * 6,
        pl.BlockSpec((4, 3, 2) + ROW, lambda n, s: (n, 0, 0, 0, 0)),
        out_like(16, 3, 4, *ROW), "pack_own")


def pack_other(scalars, own, other):
    def kernel(s, *refs):
        pack_rows(s, refs[:6], refs[7])

    def spec(a):
        return pl.BlockSpec((None, 2, 64, 256), lambda n, s: (a, 0, 0, n))

    return call(
        kernel, scalars, [other] * 6 + [own], (4,),
        [spec(a) for a in range(6)] + [pl.BlockSpec(memory_space=pl.ANY)],
        pl.BlockSpec((4, 3, 2) + ROW, lambda n, s: (n, 0, 1, 0, 0)),
        out_like(*own.shape), "pack_other", input_output_aliases={7: 0})


def other_heads(scalars, arrays):
    def kernel(s, *refs):
        for a in range(6):
            refs[6][a] = refs[a][...]

    return call(
        kernel, scalars, arrays, (2,),
        [pl.BlockSpec((2, 64, 512), lambda n, s: (0, 0, 2 * (1 - s[0]) + n))] * 6,
        pl.BlockSpec((6, 2, 64, 512), lambda n, s: (0, 0, 0, n)),
        out_like(6, 2, 64, 1024), "other_heads")


def soft_parts(s, ds):
    e = jnp.exp(s - jnp.max(s, axis=-1, keepdims=True))
    p = e * (1.0 / jnp.sum(e, axis=-1, keepdims=True))
    dp = p * (ds - jnp.sum(p * ds, axis=-1, keepdims=True))
    return p.astype(BF16), dp.astype(BF16)


def spatial_kernel(x_ref, out_ref):
    q, keys, v = [x_ref[:, a, 0].reshape(1024, LANES) for a in range(3)]
    q = q * BF16(HEAD_DIM ** -0.5)
    q_low = dot(q, shift_lanes(True)).astype(BF16)
    values = jnp.concatenate([v, dot(v, shift_lanes(False)).astype(BF16)], axis=0)
    for block in range(2):
        rows = slice(512 * block, 512 * block + 512)
        both = jnp.concatenate(soft_parts(dot_t(q_low[rows], keys), dot_t(q[rows], keys)), axis=-1)
        out_ref[8 * block:8 * block + 8, 0] = dot(both, values).astype(BF16).reshape(8, 64, LANES)


def spatial(x):
    return pl.pallas_call(
        spatial_kernel,
        grid=(4,),
        in_specs=[pl.BlockSpec((16, 3, 1) + ROW, lambda f: (0, 0, f, 0, 0))],
        out_specs=pl.BlockSpec((16, 1) + ROW, lambda f: (0, f, 0, 0)),
        out_shape=out_like(16, 4, *ROW),
        compiler_params=pltpu.CompilerParams(vmem_limit_bytes=VMEM_LIMIT),
        cost_estimate=COST,
        name="spatial",
    )(x)


def temporal_kernel(x_ref, out_ref):
    row = lax.broadcasted_iota(jnp.int32, (256, 256), 0)
    col = lax.broadcasted_iota(jnp.int32, (256, 256), 1)
    turn = jnp.where(col == (row % 16) * 16 + row // 16, 1.0, 0.0).astype(BF16)
    down, up = shift_lanes(True), shift_lanes(False)
    moved = []
    for i in range(4):
        rows = jnp.concatenate([x_ref[4 * i:4 * i + 4, a].reshape(256, LANES) for a in range(3)], axis=-1)
        rows = dot(turn, rows).astype(BF16)
        q, k, v = [rows[:, a * LANES:(a + 1) * LANES] for a in range(3)]
        q = q * BF16(HEAD_DIM ** -0.5)
        moved.append((q, dot(q, down).astype(BF16), k, v, dot(v, up).astype(BF16)))
    row = lax.broadcasted_iota(jnp.int32, (LANES, LANES), 0)
    col = lax.broadcasted_iota(jnp.int32, (LANES, LANES), 1)
    same = (row // 64) == (col // 64)
    pieces = []
    for g in range(8):
        q, q_low, k, v, v_up = [
            jnp.concatenate(
                [moved[i][m][t * 16:(t + 1) * 16] for t in (2 * g, 2 * g + 1) for i in range(4)], axis=0)
            for m in range(5)]
        scores = dot_t(jnp.concatenate([q_low, q], axis=0), k)
        p, dp = soft_parts(jnp.where(same, scores[:LANES], -jnp.inf), scores[LANES:])
        found = dot(jnp.concatenate([p, dp], axis=-1), jnp.concatenate([v, v_up], axis=0))
        pieces.append(found.astype(BF16))
    back = []
    for i in range(4):
        back.append(jnp.concatenate(
            [pieces[t // 2][(t % 2) * 64 + i * 16:(t % 2) * 64 + i * 16 + 16] for t in range(16)], axis=0))
    back = dot(turn, jnp.concatenate(back, axis=-1)).astype(BF16)
    for i in range(4):
        out_ref[4 * i:4 * i + 4] = back[:, i * LANES:(i + 1) * LANES].reshape(4, 4, 16, LANES)


def temporal(x):
    return pl.pallas_call(
        temporal_kernel,
        grid=(4,),
        in_specs=[pl.BlockSpec((16, 3, 4, 16, LANES), lambda t: (0, 0, 0, t, 0))],
        out_specs=pl.BlockSpec((16, 4, 16, LANES), lambda t: (0, 0, t, 0)),
        out_shape=out_like(16, 4, *ROW),
        compiler_params=pltpu.CompilerParams(vmem_limit_bytes=VMEM_LIMIT),
        cost_estimate=COST,
        name="temporal",
    )(x)


def add_round(a, b):
    return (a.astype(F32) + b.astype(F32)).astype(BF16)


def finish(scalars, value, other):
    def kernel(s, value_ref, other_ref, out_ref, d_out_ref):
        swap = swap_lanes()
        side = pl.program_id(0) // 2
        flip = jnp.where(side == 0, s[1], s[2])
        rows = []
        for pair in range(4):
            halves = []
            for half in range(2):
                d = (2 * pair + half) ^ flip
                halves.append(jnp.where(side == 0, value_ref[d].reshape(128, LANES), other_ref[d].reshape(128, LANES)))
            rows.append(jnp.concatenate(halves, axis=-1))
        rows = dot(jnp.concatenate(rows, axis=0), swap).astype(BF16)
        for pair in range(4):
            for i, ref in ((0, out_ref), (1, d_out_ref)):
                ref[:, :, pair * LANES:(pair + 1) * LANES] = (
                    rows[128 * pair:128 * pair + 128, i * LANES:(i + 1) * LANES].reshape(2, 64, LANES))

    block = (8, 2) + ROW
    result = pl.BlockSpec((2, 64, 512), lambda n, s: (0, 0, 2 * ((n // 2) ^ s[0]) + n % 2))
    return call(
        kernel, scalars, [value, other], (4,),
        [pl.BlockSpec(block, lambda n, s: (jnp.minimum(n, 1), 0, 0, 0)),
         pl.BlockSpec(block, lambda n, s: (jnp.maximum(n - 2, 0), 0, 0, 0))],
        [result, result], [out_like(2, 64, 2048)] * 2, "finish")


def body(*arrays):
    arrays = list(arrays)
    time = lax.axis_index("tm")
    core, zh3 = time % 2, 3 * ((time // 2) % 2)
    scalars = jnp.stack([core, zh3 * (1 - core), zh3 * core]).astype(jnp.int32)
    other = swap_cores(other_heads(scalars, arrays))
    packed = pack_other(scalars, pack_own(scalars, arrays), other)

    def lead(x):
        return exchange(x, "space"), jnp.zeros((16, 4) + ROW, BF16)

    def follow(x):
        return x, exchange(temporal(exchange(x, "time")), "time")

    def lead_rest(x, _):
        found = exchange(temporal(exchange(x, "mirrored")), "mirrored")
        return exchange(add_round(spatial(x), found), "space")

    def follow_rest(x, found):
        return add_round(exchange(spatial(exchange(x, "space")), "space"), found)

    tokens, found = lax.cond(core == 0, lead, follow, packed)
    total = lax.cond(core == 0, lead_rest, follow_rest, tokens, found)
    return tuple(finish(scalars, total, swap_cores(total[:, 2:])))


def solution(mesh):
    spec = P("tm", "space", None)
    return jax.shard_map(
        body, mesh=mesh, in_specs=(spec,) * 6, out_specs=(spec,) * 2, check_vma=False)
```
